32 devices in a mesh: ctx: 8 (over z, x), head: 4 (over y, core).
Axes of the slice: x: 2, y: 2, z: 4, core: 2. Of those that a mesh axis runs over, the one named last changes fastest.
Arguments:
- activations: bfloat16 [1024, 8192], P('ctx', 'head'), may hold values from -6 to 6
- adapter_down: bfloat16 [8192, 768], P('head'), may hold values from -0.0625 to 0.0625
- adapter_ids: int32 [1024, 2], P('ctx'), may hold values from 0 to 7, all different within a row
- adapter_weight: float32 [1024, 2], P('ctx'), may hold values from 0.05 to 0.95, as said below
- query_base: bfloat16 [1024, 8192], P('ctx', 'head'), may hold values from -110 to 110
- key_base: bfloat16 [1024, 1024], P('ctx', 'head'), may hold values from -6 to 6
- value_base: bfloat16 [1024, 1024], P('ctx', 'head'), may hold values from -6 to 6
- up_query: bfloat16 [256, 8192], P(None, 'head'), may hold values from -1 to 1
- up_key: bfloat16 [256, 1024], P(None, 'head'), may hold values from -1 to 1
- up_value: bfloat16 [256, 1024], P(None, 'head'), may hold values from -1 to 1
Outputs:
- attended: bfloat16 [1024, 8192], P('ctx', 'head')
The draws below stay inside these ranges and needn't reach their ends.
Inputs may be any that keep to these rules, and one draw needn't show every extreme that they name: `adapter_weight`: each row holds two weights that sum to one, the first the larger.
All inputs are finite; a program needn't handle non-finite values.
Results may differ from the reference program's by a relative error of at most 0.029.
Values may be sent and summed in bfloat16 or wider, within the bound.
A program may use at most 64 MiB of HBM per device.

```python
import math
import jax
import jax.numpy as jnp
from jax import lax

D = 8192
QH = 64
KVH = 8
HD = 128
ADAPTERS = 8
RANK = 32
TOKENS = 1024


def draw_adapter_weight(key, part):
    key = jax.random.fold_in(key, 5)
    leading = jax.random.uniform(key, (TOKENS, 1), jnp.float32, 0.5, 0.95)
    return jnp.concatenate([leading, 1.0 - leading], axis=1)


def draw_query_base(key, part):
    key = jax.random.fold_in(key, 11)
    shape_key = jax.random.fold_in(key, 0)
    values = jax.random.truncated_normal(shape_key, -6.0, 6.0, (TOKENS, QH * HD), jnp.float32)
    return values.astype(jnp.bfloat16)


def steps_of(stream_key, extent, cuts, smallest, high):
    loudness, own = 1.0, jax.random.fold_in(stream_key, 6)
    for position, shards_of in cuts:
        heights = jnp.exp(jax.random.uniform(jax.random.fold_in(own, position), (shards_of,), jnp.float32, smallest / len(cuts), high / len(cuts)))
        loudness = loudness * jnp.repeat(heights, extent[position] // shards_of).reshape([-1 if axis == position else 1 for axis in range(len(extent))])
    return loudness


def different_ones(stream_key, rows, amount, top, lift):
    order = jax.random.permutation(jax.random.fold_in(stream_key, 1), amount)
    pull = order
    for power in range(3):
        pull = pull * pull // amount
    pull = pull * lift // amount
    tickets = jax.random.randint(jax.random.fold_in(stream_key, 2), (rows, amount), 0, 4096) + pull
    fixed_rows = jax.random.permutation(jax.random.fold_in(stream_key, 3), rows)[jnp.arange(amount) % rows]
    tickets = jnp.where(jnp.arange(rows)[:, None] == fixed_rows[None, :], 1 << 14, tickets)
    priority = tickets * amount + jnp.arange(amount)
    return lax.top_k(priority.astype(jnp.int32), top)[1].astype(jnp.int32)


def centred(stream_key, extent, width, bound, shards=(), held_as=jnp.bfloat16):
    result = jax.random.normal(stream_key, extent, jnp.float32) * width
    if len(shards) > 0:
        result = steps_of(stream_key, extent, shards, -0.22, 0.18) * result
    return jnp.clip(result, min=-bound, max=bound).astype(held_as)


def setup_inputs(seed: int = 0) -> dict:
    seeds = jax.random.split(jax.random.key(seed), 11)
    activations = centred(seeds[0], (TOKENS, D), 1.0, 6.0, ((0, 8), (1, 4)))
    adapter_down = centred(seeds[1], (D, 3 * ADAPTERS * RANK), D ** -0.5, 0.0625, ((0, 4),))
    adapter_ids = different_ones(seeds[2], TOKENS, ADAPTERS, 2, 4096)
    adapter_weight = draw_adapter_weight(jax.random.fold_in(seeds[10], 71), 0)
    query_base = draw_query_base(jax.random.fold_in(seeds[10], 71), 0)
    key_base = centred(seeds[5], (TOKENS, KVH * HD), 1.0, 6.0, ((0, 8), (1, 4)))
    value_base = centred(seeds[6], (TOKENS, KVH * HD), 1.0, 6.0, ((0, 8), (1, 4)))
    up_query = centred(seeds[7], (ADAPTERS * RANK, QH * HD), RANK ** -0.5, 1.0, ((1, 4),))
    up_key = centred(seeds[8], (ADAPTERS * RANK, KVH * HD), RANK ** -0.5, 1.0, ((1, 4),))
    up_value = centred(seeds[9], (ADAPTERS * RANK, KVH * HD), RANK ** -0.5, 1.0, ((1, 4),))
    return dict(activations=activations, adapter_down=adapter_down, adapter_ids=adapter_ids, adapter_weight=adapter_weight, query_base=query_base, key_base=key_base, value_base=value_base, up_query=up_query, up_key=up_key, up_value=up_value)


rope_base = 500000.0
floor_value = -1e+30

def rotate(values, positions):
    row_count = values.shape[0]
    heads = values.shape[1] // HD
    half_width = HD // 2
    inverse = jnp.exp(jnp.arange(half_width, dtype=jnp.float32) * (-2.0 * math.log(rope_base) / HD))
    angles = positions.astype(jnp.float32)[:, None] * inverse[None, :]
    cosine = jnp.cos(angles)[:, None, :]
    sine = jnp.sin(angles)[:, None, :]
    shaped = values.reshape(row_count, heads, HD)
    first_half = shaped[:, :, :half_width]
    second_half = shaped[:, :, half_width:]
    turned = jnp.concatenate([first_half * cosine - second_half * sine, second_half * cosine + first_half * sine], axis=2)
    return turned.reshape(row_count, heads * HD)

def mixture(adapter_ids, adapter_weight):
    labels = jnp.arange(ADAPTERS, dtype=jnp.int32)
    matches = (adapter_ids[:, :, None] == labels[None, None, :]).astype(jnp.float32)
    return lax.optimization_barrier(jnp.sum(matches * adapter_weight[:, :, None], axis=1))

def gate_rows(low_rank, coefficient):
    row_count = low_rank.shape[0]
    shaped = low_rank.reshape(row_count, 3, ADAPTERS, RANK)
    gated = shaped * coefficient[:, None, :, None]
    return gated.astype(jnp.bfloat16).reshape(row_count, 3 * ADAPTERS * RANK)

def project(gated, query_base, key_base, value_base, up_query, up_key, up_value, positions):
    span = ADAPTERS * RANK
    query_raw = query_base.astype(jnp.float32) + jnp.dot(gated[:, :span], up_query, preferred_element_type=jnp.float32)
    key_raw = key_base.astype(jnp.float32) + jnp.dot(gated[:, span:2 * span], up_key, preferred_element_type=jnp.float32)
    value_raw = value_base.astype(jnp.float32) + jnp.dot(gated[:, 2 * span:], up_value, preferred_element_type=jnp.float32)
    query = rotate(query_raw, positions).astype(jnp.bfloat16)
    keys = rotate(key_raw, positions).astype(jnp.bfloat16)
    return (query, keys, value_raw.astype(jnp.bfloat16))

def reference(activations, adapter_down, adapter_ids, adapter_weight, query_base, key_base, value_base, up_query, up_key, up_value):
    low_rank = jnp.dot(activations, adapter_down, preferred_element_type=jnp.float32)
    gated = gate_rows(low_rank, mixture(adapter_ids, adapter_weight))
    positions = jnp.arange(TOKENS, dtype=jnp.int32)
    query, keys, values = project(gated, query_base, key_base, value_base, up_query, up_key, up_value, positions)
    group_size = QH // KVH
    scale_factor = 1.0 / math.sqrt(HD)
    query_wide = lax.optimization_barrier(query).astype(jnp.float32).reshape(TOKENS, KVH, group_size, HD).transpose(1, 2, 0, 3)
    key_wide = lax.optimization_barrier(keys).astype(jnp.float32).reshape(TOKENS, KVH, HD).transpose(1, 0, 2)
    value_wide = lax.optimization_barrier(values).astype(jnp.float32).reshape(TOKENS, KVH, HD).transpose(1, 0, 2)
    block_rows = math.gcd(TOKENS, 512)
    block_count = TOKENS // block_rows

    def per_head(operands):
        query_head, key_head, value_head = operands

        def per_block(block_start):
            query_block = lax.dynamic_slice_in_dim(query_head, block_start, block_rows, 1)
            query_pos = block_start + jnp.arange(block_rows, dtype=jnp.int32)
            scores = jnp.einsum('gqd,kd->gqk', query_block, key_head, precision=lax.Precision.HIGHEST) * scale_factor
            allowed = (query_pos[:, None] >= positions[None, :])[None]
            scores = jnp.where(allowed, scores, floor_value)
            top_score = lax.optimization_barrier(jnp.max(scores, axis=2, keepdims=True))
            expo = jnp.where(allowed, jnp.exp(scores - top_score), 0.0)
            total = lax.optimization_barrier(jnp.sum(expo, axis=2, keepdims=True))
            rounded = lax.optimization_barrier(expo.astype(jnp.bfloat16)).astype(jnp.float32)
            summed = jnp.einsum('gqk,kd->gqd', rounded, value_head, precision=lax.Precision.HIGHEST)
            return (summed / total).astype(jnp.bfloat16)
        starts = jnp.arange(block_count, dtype=jnp.int32) * block_rows
        return lax.map(per_block, starts)
    outputs = lax.map(per_head, (query_wide, key_wide, value_wide))
    return outputs.transpose(1, 3, 0, 2, 4).reshape(TOKENS, QH * HD)
```

```python
import functools
import math

import jax
import jax.numpy as jnp
import numpy as np
from jax import lax
from jax.experimental import pallas as pl
from jax.experimental.pallas import tpu as pltpu
from jax.sharding import PartitionSpec as P

HD = 128
ADAPTERS = 8
RANK = 32
SPAN = ADAPTERS * RANK
ROPE_BASE = 500000.0
MASKED = -1e30
MESH = pl.DeviceIdType.MESH
CHUNKS = 4


def roll_lanes(values, shift):
    return pltpu.roll(values, shift, 1)


def spread(values):
    values = values + roll_lanes(values, 64)
    return values + roll_lanes(values, 32)


def kernel(
    n_ctx,
    n_head,
    act_hbm,
    down_hbm,
    ids_ref,
    weight_ref,
    qbase_hbm,
    kbase_hbm,
    vbase_hbm,
    upq_hbm,
    upk_hbm,
    upv_hbm,
    inverse_ref,
    out_ref,
    act,
    down,
    qbase,
    kbase,
    vbase,
    upq,
    upk,
    upv,
    low_send,
    low_recv,
    kv,
    qs,
    top,
    total,
    accum,
    cos_tab,
    sin_tab,
    in_sems,
    low_send_sems,
    low_recv_sems,
    lane_send_sems,
    cross_send_sems,
    recv_sems,
):
    ctx = lax.axis_index("ctx")
    head = lax.axis_index("head")
    z = ctx // 2
    x = ctx % 2
    n_z = n_ctx // 2
    rows, features = act.shape
    local_kv = kbase.shape[1] // HD
    group = qbase.shape[1] // HD // local_kv
    kv_width = local_kv * HD
    other = 2 * z + 1 - x

    part = features // CHUNKS
    loads = [pltpu.make_async_copy(act_hbm, act, in_sems.at[0])]
    for i in range(CHUNKS):
        piece = pl.ds(i * part, part)
        loads.append(pltpu.make_async_copy(down_hbm.at[piece], down.at[piece], in_sems.at[1 + i]))
    rest = [
        pltpu.make_async_copy(src, dst, in_sems.at[1 + CHUNKS + i])
        for i, (src, dst) in enumerate(
            ((kbase_hbm, kbase), (vbase_hbm, vbase), (upk_hbm, upk), (upv_hbm, upv), (qbase_hbm, qbase), (upq_hbm, upq))
        )
    ]
    for load in loads + rest:
        load.start()

    barrier = pltpu.get_barrier_semaphore()
    for step in range(1, n_head):
        pl.semaphore_signal(
            barrier, inc=1, device_id={"ctx": ctx, "head": lax.rem(head + step, n_head)}, device_id_type=MESH
        )
    pl.semaphore_signal(barrier, inc=1, device_id={"ctx": other, "head": head}, device_id_type=MESH)

    @pl.when(z > 0)
    def _():
        pl.semaphore_signal(barrier, inc=1, device_id={"ctx": ctx - 2, "head": head}, device_id_type=MESH)

    @pl.when(z < n_z - 1)
    def _():
        pl.semaphore_signal(barrier, inc=1, device_id={"ctx": ctx + 2, "head": head}, device_id_type=MESH)

    loads[0].wait()
    low = None
    for i in range(CHUNKS):
        loads[1 + i].wait()
        piece = pl.ds(i * part, part)
        term = jnp.dot(act[:, piece], down[piece, :], preferred_element_type=jnp.float32)
        low = term if low is None else low + term

    lane = lax.broadcasted_iota(jnp.int32, (rows, HD), 1)
    group_of = lane // RANK
    masks = []
    for j in range(2):
        chosen = ids_ref[:, j : j + 1]
        masks.append((chosen == group_of, chosen == group_of + 4))
    packs = []
    for p in range(3):
        for j in range(2):
            first, second = masks[j]
            left = low[:, p * SPAN : p * SPAN + HD]
            right = low[:, p * SPAN + HD : (p + 1) * SPAN]
            packs.append(spread(jnp.where(first, left, jnp.where(second, right, 0.0))))
    half = rows // 2
    upper = jnp.where(
        group_of == 0, packs[2], jnp.where(group_of == 1, packs[3], jnp.where(group_of == 2, packs[4], packs[5]))
    )
    half_group = group_of[:half]
    lower = jnp.where(
        half_group == 0,
        packs[0][:half],
        jnp.where(half_group == 1, packs[1][:half], jnp.where(half_group == 2, packs[0][half:], packs[1][half:])),
    )
    compact = jnp.concatenate([upper, lower], axis=0)
    low_send[...] = compact.astype(jnp.bfloat16)

    neighbours = n_head + (z > 0).astype(jnp.int32) + (z < n_z - 1).astype(jnp.int32)
    pl.semaphore_wait(barrier, neighbours)

    low_copies = []
    for step in range(n_head - 1, 0, -1):
        peer = lax.rem(head + step, n_head)
        copy = pltpu.make_async_remote_copy(
            src_ref=low_send,
            dst_ref=low_recv.at[head],
            send_sem=low_send_sems.at[step],
            recv_sem=low_recv_sems.at[head],
            device_id={"ctx": ctx, "head": peer},
            device_id_type=MESH,
        )
        copy.start()
        low_copies.append(copy)

    spot = lax.broadcasted_iota(jnp.int32, (rows, HD), 0) + ctx * rows
    angles = spot.astype(jnp.float32) * inverse_ref[...]
    cos_tab[...] = jnp.cos(angles)
    sine = jnp.sin(angles)
    sin_tab[...] = jnp.where(lane < HD // 2, -sine, sine)

    for load in rest:
        load.wait()
    for step in range(1, n_head):
        peer = lax.rem(head + step, n_head)
        pltpu.make_async_copy(low_recv.at[peer], low_recv.at[peer], low_recv_sems.at[peer]).wait()
        compact = compact + low_recv[peer].astype(jnp.float32)

    upper, lower = compact[:rows], compact[rows:]
    pieces = [
        jnp.concatenate(
            [
                spread(jnp.where(half_group == j, lower, 0.0)),
                spread(jnp.where(half_group == j + 2, lower, 0.0)),
            ],
            axis=0,
        )
        for j in range(2)
    ]
    pieces += [spread(jnp.where(group_of == k, upper, 0.0)) for k in range(4)]

    def gated_of(p):
        first = weight_ref[:, 0:1] * pieces[2 * p]
        second = weight_ref[:, 1:2] * pieces[2 * p + 1]
        sides = [
            jnp.where(masks[0][side], first, jnp.where(masks[1][side], second, 0.0)) for side in range(2)
        ]
        return jnp.concatenate(sides, axis=1).astype(jnp.bfloat16)

    def rotated(values):
        return (values * cos_tab[...] + roll_lanes(values, HD // 2) * sin_tab[...]).astype(jnp.bfloat16)

    key_raw = kbase[...].astype(jnp.float32) + jnp.dot(gated_of(1), upk[...], preferred_element_type=jnp.float32)
    for g in range(local_kv):
        kv[ctx, :, g * HD : (g + 1) * HD] = rotated(key_raw[:, g * HD : (g + 1) * HD])
    value = vbase[...].astype(jnp.float32) + jnp.dot(gated_of(2), upv[...], preferred_element_type=jnp.float32)
    kv[ctx, :, kv_width:] = value.astype(jnp.bfloat16)

    def lane_copy(block):
        return pltpu.make_async_remote_copy(
            src_ref=kv.at[block],
            dst_ref=kv.at[block],
            send_sem=lane_send_sems.at[block],
            recv_sem=recv_sems.at[block],
            device_id={"ctx": lax.rem(ctx + 2, n_ctx), "head": head},
            device_id_type=MESH,
        )

    def cross_copy(block):
        return pltpu.make_async_remote_copy(
            src_ref=kv.at[block],
            dst_ref=kv.at[block],
            send_sem=cross_send_sems.at[block],
            recv_sem=recv_sems.at[block],
            device_id={"ctx": other, "head": head},
            device_id_type=MESH,
        )

    def arrived(block):
        pltpu.make_async_copy(kv.at[block], kv.at[block], recv_sems.at[block]).wait()

    @pl.when(x == 0)
    def _():
        cross_copy(ctx).start()

    @pl.when(z < n_z - 1)
    def _():
        lane_copy(ctx).start()

    gated = gated_of(0)
    for g in range(local_kv):
        for h in range(group):
            cols = pl.ds((g * group + h) * HD, HD)
            raw = qbase[:, cols].astype(jnp.float32) + jnp.dot(
                gated, upq[:, cols], preferred_element_type=jnp.float32
            )
            qs[g, h * rows : (h + 1) * rows, :] = rotated(raw)

    factor = math.log2(math.e) / math.sqrt(HD)
    strip = 2 * rows

    def attend(block, count, diagonal):
        for g in range(local_kv):
            keys = kv[pl.ds(block, count), :, g * HD : (g + 1) * HD].reshape(count * rows, HD)
            vals = kv[pl.ds(block, count), :, kv_width + g * HD : kv_width + (g + 1) * HD].reshape(count * rows, HD)
            for c in range(group * rows // strip):
                span = pl.ds(c * strip, strip)
                scores = (
                    lax.dot_general(
                        qs[g, span, :], keys, (((1,), (1,)), ((), ())), preferred_element_type=jnp.float32
                    )
                    * factor
                )
                if diagonal:
                    row = lax.broadcasted_iota(jnp.int32, (strip, rows), 0) % rows
                    col = lax.broadcasted_iota(jnp.int32, (strip, rows), 1)
                    scores = jnp.where(row >= col, scores, MASKED)
                peak = jnp.max(scores, axis=1, keepdims=True)
                if diagonal:
                    new_top = jnp.broadcast_to(peak, (strip, HD))
                else:
                    old_top = top[g, span, :]
                    new_top = jnp.maximum(old_top, peak)
                    shrink = jnp.exp2(old_top - new_top)
                top[g, span, :] = new_top
                sums = None
                expos = []
                for k in range(count):
                    expo = jnp.exp2(scores[:, k * rows : (k + 1) * rows] - new_top)
                    sums = expo if sums is None else sums + expo
                    expos.append(expo.astype(jnp.bfloat16))
                expo = expos[0] if count == 1 else jnp.concatenate(expos, axis=1)
                summed = jnp.dot(expo, vals, preferred_element_type=jnp.float32)
                if diagonal:
                    total[g, span, :] = sums
                    accum[g, span, :] = summed
                else:
                    total[g, span, :] = total[g, span, :] * shrink + sums
                    accum[g, span, :] = accum[g, span, :] * shrink + summed

    attend(ctx, 1, True)

    def pass_on(block):
        arrived(block)

        @pl.when(z < n_z - 1)
        def _():
            lane_copy(block).start()

        cross_copy(block).start()

    @pl.when(z > 0)
    def _():
        pass_on(ctx - 2)

    @pl.when(x == 1)
    def _():
        arrived(ctx - 1)
        attend(ctx - 1, 1, False)

    def pair_step(step, carry):
        @pl.when(step < z)
        def _():
            pass_on(ctx - 2 * step - 2)

        arrived(other - 2 * step)
        attend(2 * (z - step), 2, False)
        return carry

    lax.fori_loop(1, z + 1, pair_step, 0)

    for g in range(local_kv):
        for h in range(group):
            span = pl.ds(h * rows, rows)
            whole = jnp.sum(total[g, span, :], axis=1, keepdims=True)
            cols = pl.ds((g * group + h) * HD, HD)
            out_ref[:, cols] = (accum[g, span, :] / whole).astype(jnp.bfloat16)

    for copy in low_copies:
        copy.wait_send()

    @pl.when(x == 0)
    def _():
        cross_copy(ctx).wait_send()

    @pl.when(z < n_z - 1)
    def _():
        lane_copy(ctx).wait_send()

    def drain(step, carry):
        block = ctx - 2 * step
        cross_copy(block).wait_send()

        @pl.when(z < n_z - 1)
        def _():
            lane_copy(block).wait_send()

        return carry

    lax.fori_loop(1, z + 1, drain, 0)


def on_device(
    n_ctx,
    n_head,
    activations,
    adapter_down,
    adapter_ids,
    adapter_weight,
    query_base,
    key_base,
    value_base,
    up_query,
    up_key,
    up_value,
):
    rows = activations.shape[0]
    width = query_base.shape[1]
    kv_width = key_base.shape[1]
    local_kv = kv_width // HD
    stacked = rows * (width // kv_width)
    exponent = np.arange(HD // 2, dtype=np.float32) * np.float32(-2.0 * math.log(ROPE_BASE) / HD)
    inverse = np.exp(np.concatenate([exponent, exponent])).astype(np.float32)[None, :]
    bf16, f32 = jnp.bfloat16, jnp.float32
    big = (activations, adapter_down, query_base, key_base, value_base, up_query, up_key, up_value)
    anywhere = pl.BlockSpec(memory_space=pl.ANY)
    local = pl.BlockSpec(memory_space=pltpu.VMEM)
    return pl.pallas_call(
        functools.partial(kernel, n_ctx, n_head),
        out_shape=jax.ShapeDtypeStruct((rows, width), bf16),
        in_specs=[anywhere, anywhere, local, local] + [anywhere] * 6 + [local],
        out_specs=local,
        scratch_shapes=[pltpu.VMEM(array.shape, array.dtype) for array in big]
        + [
            pltpu.VMEM((rows + rows // 2, HD), bf16),
            pltpu.VMEM((n_head, rows + rows // 2, HD), bf16),
            pltpu.VMEM((n_ctx, rows, 2 * kv_width), bf16),
            pltpu.VMEM((local_kv, stacked, HD), bf16),
            pltpu.VMEM((local_kv, stacked, HD), f32),
            pltpu.VMEM((local_kv, stacked, HD), f32),
            pltpu.VMEM((local_kv, stacked, HD), f32),
            pltpu.VMEM((rows, HD), f32),
            pltpu.VMEM((rows, HD), f32),
            pltpu.SemaphoreType.DMA((7 + CHUNKS,)),
            pltpu.SemaphoreType.DMA((n_head,)),
            pltpu.SemaphoreType.DMA((n_head,)),
            pltpu.SemaphoreType.DMA((n_ctx,)),
            pltpu.SemaphoreType.DMA((n_ctx,)),
            pltpu.SemaphoreType.DMA((n_ctx,)),
        ],
        compiler_params=pltpu.CompilerParams(
            collective_id=0, has_side_effects=True, vmem_limit_bytes=48 * 1024 * 1024
        ),
        name="lora_attention",
    )(
        activations,
        adapter_down,
        adapter_ids,
        adapter_weight,
        query_base,
        key_base,
        value_base,
        up_query,
        up_key,
        up_value,
        inverse,
    )


def solution(mesh):
    in_specs = (
        P("ctx", "head"),
        P("head", None),
        P("ctx", None),
        P("ctx", None),
        P("ctx", "head"),
        P("ctx", "head"),
        P("ctx", "head"),
        P(None, "head"),
        P(None, "head"),
        P(None, "head"),
    )
    return jax.shard_map(
        functools.partial(on_device, mesh.shape["ctx"], mesh.shape["head"]),
        mesh=mesh,
        in_specs=in_specs,
        out_specs=P("ctx", "head"),
        check_vma=False,
    )
```

```python
import functools
import math

import jax
import jax.numpy as jnp
import numpy as np
from jax import lax
from jax.experimental import pallas as pl
from jax.experimental.pallas import tpu as pltpu
from jax.sharding import PartitionSpec as P

HD = 128
ADAPTERS = 8
RANK = 32
SPAN = ADAPTERS * RANK
ROPE_BASE = 500000.0
MASKED = -1e30
MESH = pl.DeviceIdType.MESH
CHUNKS = 4


def roll_lanes(values, shift):
    return pltpu.roll(values, shift, 1)


def spread(values):
    values = values + roll_lanes(values, 64)
    return values + roll_lanes(values, 32)


def columns(row, rows):
    return jnp.broadcast_to(row, (HD, rows)).T


def kernel(
    n_ctx,
    n_head,
    act_hbm,
    down_hbm,
    ids_hbm,
    weight_hbm,
    qbase_hbm,
    kbase_hbm,
    vbase_hbm,
    upq_hbm,
    upk_hbm,
    upv_hbm,
    inverse_hbm,
    out_ref,
    act,
    down,
    ids_ref,
    weight_ref,
    qbase,
    kbase,
    vbase,
    upq,
    upk,
    upv,
    inverse_ref,
    low_send,
    low_recv,
    kv,
    qs,
    top,
    total,
    accum,
    cos_tab,
    sin_tab,
    in_sems,
    low_send_sems,
    low_recv_sems,
    lane_send_sems,
    cross_send_sems,
    recv_sems,
):
    ctx = lax.axis_index("ctx")
    head = lax.axis_index("head")
    z = ctx // 2
    x = ctx % 2
    n_z = n_ctx // 2
    rows, features = act.shape
    local_kv = kbase.shape[1] // HD
    group = qbase.shape[1] // HD // local_kv
    other = 2 * z + 1 - x

    part = features // CHUNKS
    loads = [pltpu.make_async_copy(act_hbm, act, in_sems.at[0])]
    for i in range(CHUNKS):
        piece = pl.ds(i * part, part)
        loads.append(pltpu.make_async_copy(down_hbm.at[piece], down.at[piece], in_sems.at[1 + i]))
    rest = [
        pltpu.make_async_copy(src, dst, in_sems.at[1 + CHUNKS + i])
        for i, (src, dst) in enumerate(
            ((ids_hbm, ids_ref), (weight_hbm, weight_ref), (inverse_hbm, inverse_ref), (kbase_hbm, kbase), (vbase_hbm, vbase), (upk_hbm, upk), (upv_hbm, upv), (qbase_hbm, qbase), (upq_hbm, upq))
        )
    ]
    small, rest = rest[:3], rest[3:]
    for load in small + loads + rest:
        load.start()

    barrier = pltpu.get_barrier_semaphore()
    for step in range(1, n_head):
        pl.semaphore_signal(
            barrier, inc=1, device_id={"ctx": ctx, "head": lax.rem(head + step, n_head)}, device_id_type=MESH
        )
    pl.semaphore_signal(barrier, inc=1, device_id={"ctx": other, "head": head}, device_id_type=MESH)

    @pl.when(z > 0)
    def _():
        pl.semaphore_signal(barrier, inc=1, device_id={"ctx": ctx - 2, "head": head}, device_id_type=MESH)

    @pl.when(z < n_z - 1)
    def _():
        pl.semaphore_signal(barrier, inc=1, device_id={"ctx": ctx + 2, "head": head}, device_id_type=MESH)

    loads[0].wait()
    low = None
    for i in range(CHUNKS):
        loads[1 + i].wait()
        piece = pl.ds(i * part, part)
        term = jnp.dot(act[:, piece], down[piece, :], preferred_element_type=jnp.float32)
        low = term if low is None else low + term

    for load in small:
        load.wait()
    lane = lax.broadcasted_iota(jnp.int32, (rows, HD), 1)
    group_of = lane // RANK
    group_value = group_of.astype(jnp.float32)
    masks = []
    for j in range(2):
        chosen = columns(ids_ref[j : j + 1, :].astype(jnp.float32), rows)
        masks.append((chosen == group_value, chosen == group_value + 4.0))
    packs = []
    for p in range(3):
        for j in range(2):
            first, second = masks[j]
            left = low[:, p * SPAN : p * SPAN + HD]
            right = low[:, p * SPAN + HD : (p + 1) * SPAN]
            packs.append(spread(jnp.where(first, left, jnp.where(second, right, 0.0))))
    half = rows // 2
    upper = jnp.where(
        group_of == 0, packs[2], jnp.where(group_of == 1, packs[3], jnp.where(group_of == 2, packs[4], packs[5]))
    )
    half_group = group_of[:half]
    lower = jnp.where(
        half_group == 0,
        packs[0][:half],
        jnp.where(half_group == 1, packs[1][:half], jnp.where(half_group == 2, packs[0][half:], packs[1][half:])),
    )
    compact = jnp.concatenate([upper, lower], axis=0)
    low_send[...] = compact.astype(jnp.bfloat16)

    neighbours = n_head + (z > 0).astype(jnp.int32) + (z < n_z - 1).astype(jnp.int32)
    pl.semaphore_wait(barrier, neighbours)

    low_copies = []
    for step in range(n_head - 1, 0, -1):
        peer = lax.rem(head + step, n_head)
        copy = pltpu.make_async_remote_copy(
            src_ref=low_send,
            dst_ref=low_recv.at[head],
            send_sem=low_send_sems.at[step],
            recv_sem=low_recv_sems.at[head],
            device_id={"ctx": ctx, "head": peer},
            device_id_type=MESH,
        )
        copy.start()
        low_copies.append(copy)

    spot = lax.broadcasted_iota(jnp.int32, (rows, HD), 0) + ctx * rows
    angles = spot.astype(jnp.float32) * inverse_ref[...]
    cos_tab[...] = jnp.cos(angles)
    sine = jnp.sin(angles)
    sin_tab[...] = jnp.where(lane < HD // 2, -sine, sine)

    for load in rest:
        load.wait()
    for step in range(1, n_head):
        peer = lax.rem(head + step, n_head)
        pltpu.make_async_copy(low_recv.at[peer], low_recv.at[peer], low_recv_sems.at[peer]).wait()
        compact = compact + low_recv[peer].astype(jnp.float32)

    upper, lower = compact[:rows], compact[rows:]
    pieces = [
        jnp.concatenate(
            [
                spread(jnp.where(half_group == j, lower, 0.0)),
                spread(jnp.where(half_group == j + 2, lower, 0.0)),
            ],
            axis=0,
        )
        for j in range(2)
    ]
    pieces += [spread(jnp.where(group_of == k, upper, 0.0)) for k in range(4)]

    shares = [columns(weight_ref[j : j + 1, :], rows) for j in range(2)]

    def gated_of(p):
        first = shares[0] * pieces[2 * p]
        second = shares[1] * pieces[2 * p + 1]
        sides = [
            jnp.where(masks[0][side], first, jnp.where(masks[1][side], second, 0.0)) for side in range(2)
        ]
        return jnp.concatenate(sides, axis=1).astype(jnp.bfloat16)

    def rotated(values):
        return (values * cos_tab[...] + roll_lanes(values, HD // 2) * sin_tab[...]).astype(jnp.bfloat16)

    key_raw = kbase[...].astype(jnp.float32) + jnp.dot(gated_of(1), upk[...], preferred_element_type=jnp.float32)
    for g in range(local_kv):
        kv[ctx, g, :, :HD] = rotated(key_raw[:, g * HD : (g + 1) * HD])
    value = vbase[...].astype(jnp.float32) + jnp.dot(gated_of(2), upv[...], preferred_element_type=jnp.float32)
    for g in range(local_kv):
        kv[ctx, g, :, HD:] = value[:, g * HD : (g + 1) * HD].astype(jnp.bfloat16)

    def lane_copy(block, g):
        return pltpu.make_async_remote_copy(
            src_ref=kv.at[block, g],
            dst_ref=kv.at[block, g],
            send_sem=lane_send_sems.at[block, g],
            recv_sem=recv_sems.at[block, g],
            device_id={"ctx": lax.rem(ctx + 2, n_ctx), "head": head},
            device_id_type=MESH,
        )

    def cross_copy(block, g):
        return pltpu.make_async_remote_copy(
            src_ref=kv.at[block, g],
            dst_ref=kv.at[block, g],
            send_sem=cross_send_sems.at[block, g],
            recv_sem=recv_sems.at[block, g],
            device_id={"ctx": other, "head": head},
            device_id_type=MESH,
        )

    def arrived(block, g):
        pltpu.make_async_copy(kv.at[block, g], kv.at[block, g], recv_sems.at[block, g]).wait()

    for g in range(local_kv):

        @pl.when(x == 0)
        def _():
            cross_copy(ctx, g).start()

        @pl.when(z < n_z - 1)
        def _():
            lane_copy(ctx, g).start()

    gated = gated_of(0)
    for g in range(local_kv):
        for h in range(group):
            cols = pl.ds((g * group + h) * HD, HD)
            raw = qbase[:, cols].astype(jnp.float32) + jnp.dot(
                gated, upq[:, cols], preferred_element_type=jnp.float32
            )
            qs[g, h * rows : (h + 1) * rows, :] = rotated(raw)

    factor = math.log2(math.e) / math.sqrt(HD)
    strip = 2 * rows

    def attend(block, count, diagonal, g):
        keys = kv[pl.ds(block, count), g, :, :HD].reshape(count * rows, HD)
        vals = kv[pl.ds(block, count), g, :, HD:].reshape(count * rows, HD)
        for c in range(group * rows // strip):
            span = pl.ds(c * strip, strip)
            scores = (
                lax.dot_general(
                    qs[g, span, :], keys, (((1,), (1,)), ((), ())), preferred_element_type=jnp.float32
                )
                * factor
            )
            if diagonal:
                row = lax.broadcasted_iota(jnp.int32, (strip, rows), 0) % rows
                col = lax.broadcasted_iota(jnp.int32, (strip, rows), 1)
                scores = jnp.where(row >= col, scores, MASKED)
            peak = jnp.max(scores, axis=1, keepdims=True)
            if diagonal:
                new_top = jnp.broadcast_to(peak, (strip, HD))
            else:
                old_top = top[g, span, :]
                new_top = jnp.maximum(old_top, peak)
                shrink = jnp.exp2(old_top - new_top)
            top[g, span, :] = new_top
            sums = None
            expos = []
            for k in range(count):
                expo = jnp.exp2(scores[:, k * rows : (k + 1) * rows] - new_top)
                sums = expo if sums is None else sums + expo
                expos.append(expo.astype(jnp.bfloat16))
            expo = expos[0] if count == 1 else jnp.concatenate(expos, axis=1)
            summed = jnp.dot(expo, vals, preferred_element_type=jnp.float32)
            if diagonal:
                total[g, span, :] = sums
                accum[g, span, :] = summed
            else:
                total[g, span, :] = total[g, span, :] * shrink + sums
                accum[g, span, :] = accum[g, span, :] * shrink + summed

    def pass_on(block, g):
        arrived(block, g)

        @pl.when(z < n_z - 1)
        def _():
            lane_copy(block, g).start()

        cross_copy(block, g).start()

    for g in range(local_kv):
        attend(ctx, 1, True, g)

    for g in range(local_kv):

        @pl.when(z > 0)
        def _():
            pass_on(ctx - 2, g)

        @pl.when(x == 1)
        def _():
            arrived(ctx - 1, g)
            attend(ctx - 1, 1, False, g)

    def pair_step(step, carry):
        for g in range(local_kv):

            @pl.when(step < z)
            def _():
                pass_on(ctx - 2 * step - 2, g)

            arrived(other - 2 * step, g)
            attend(2 * (z - step), 2, False, g)
        return carry

    lax.fori_loop(1, z + 1, pair_step, 0)

    for g in range(local_kv):
        for h in range(group):
            span = pl.ds(h * rows, rows)
            whole = jnp.sum(total[g, span, :], axis=1, keepdims=True)
            cols = pl.ds((g * group + h) * HD, HD)
            out_ref[:, cols] = (accum[g, span, :] / whole).astype(jnp.bfloat16)

    for copy in low_copies:
        copy.wait_send()

    for g in range(local_kv):

        @pl.when(x == 0)
        def _():
            cross_copy(ctx, g).wait_send()

        @pl.when(z < n_z - 1)
        def _():
            lane_copy(ctx, g).wait_send()

    def drain(step, carry):
        block = ctx - 2 * step
        for g in range(local_kv):
            cross_copy(block, g).wait_send()

            @pl.when(z < n_z - 1)
            def _():
                lane_copy(block, g).wait_send()

        return carry

    lax.fori_loop(1, z + 1, drain, 0)


def on_device(
    n_ctx,
    n_head,
    activations,
    adapter_down,
    adapter_ids,
    adapter_weight,
    query_base,
    key_base,
    value_base,
    up_query,
    up_key,
    up_value,
):
    rows = activations.shape[0]
    width = query_base.shape[1]
    kv_width = key_base.shape[1]
    local_kv = kv_width // HD
    stacked = rows * (width // kv_width)
    exponent = np.arange(HD // 2, dtype=np.float32) * np.float32(-2.0 * math.log(ROPE_BASE) / HD)
    inverse = np.exp(np.concatenate([exponent, exponent])).astype(np.float32)[None, :]
    bf16, f32 = jnp.bfloat16, jnp.float32
    adapter_ids, adapter_weight = adapter_ids.T, adapter_weight.T
    big = (activations, adapter_down, adapter_ids, adapter_weight, query_base, key_base, value_base, up_query, up_key, up_value, inverse)
    anywhere = pl.BlockSpec(memory_space=pl.ANY)
    local = pl.BlockSpec(memory_space=pltpu.VMEM)
    return pl.pallas_call(
        functools.partial(kernel, n_ctx, n_head),
        out_shape=jax.ShapeDtypeStruct((rows, width), bf16),
        in_specs=[anywhere] * 11,
        out_specs=local,
        scratch_shapes=[pltpu.VMEM(array.shape, array.dtype) for array in big]
        + [
            pltpu.VMEM((rows + rows // 2, HD), bf16),
            pltpu.VMEM((n_head, rows + rows // 2, HD), bf16),
            pltpu.VMEM((n_ctx, local_kv, rows, 2 * HD), bf16),
            pltpu.VMEM((local_kv, stacked, HD), bf16),
            pltpu.VMEM((local_kv, stacked, HD), f32),
            pltpu.VMEM((local_kv, stacked, HD), f32),
            pltpu.VMEM((local_kv, stacked, HD), f32),
            pltpu.VMEM((rows, HD), f32),
            pltpu.VMEM((rows, HD), f32),
            pltpu.SemaphoreType.DMA((10 + CHUNKS,)),
            pltpu.SemaphoreType.DMA((n_head,)),
            pltpu.SemaphoreType.DMA((n_head,)),
            pltpu.SemaphoreType.DMA((n_ctx, local_kv)),
            pltpu.SemaphoreType.DMA((n_ctx, local_kv)),
            pltpu.SemaphoreType.DMA((n_ctx, local_kv)),
        ],
        compiler_params=pltpu.CompilerParams(
            collective_id=0, has_side_effects=True, vmem_limit_bytes=63 * 1024 * 1024
        ),
        name="lora_attention",
    )(
        activations,
        adapter_down,
        adapter_ids,
        adapter_weight,
        query_base,
        key_base,
        value_base,
        up_query,
        up_key,
        up_value,
        inverse,
    )


def solution(mesh):
    in_specs = (
        P("ctx", "head"),
        P("head", None),
        P("ctx", None),
        P("ctx", None),
        P("ctx", "head"),
        P("ctx", "head"),
        P("ctx", "head"),
        P(None, "head"),
        P(None, "head"),
        P(None, "head"),
    )
    return jax.shard_map(
        functools.partial(on_device, mesh.shape["ctx"], mesh.shape["head"]),
        mesh=mesh,
        in_specs=in_specs,
        out_specs=P("ctx", "head"),
        check_vma=False,
    )
```

```python
import functools
import math

import jax
import jax.numpy as jnp
import numpy as np
from jax import lax
from jax.experimental import pallas as pl
from jax.experimental.pallas import tpu as pltpu
from jax.sharding import PartitionSpec as P

HD = 128
ADAPTERS = 8
RANK = 32
SPAN = ADAPTERS * RANK
ROPE_BASE = 500000.0
MASKED = -1e30
MESH = pl.DeviceIdType.MESH
CHUNKS = 4


def roll_lanes(values, shift):
    return pltpu.roll(values, shift, 1)


def spread(values):
    values = values + roll_lanes(values, 64)
    return values + roll_lanes(values, 32)


def columns(row, rows):
    return jnp.broadcast_to(row, (HD, rows)).T


def kernel(
    n_ctx,
    n_head,
    act_hbm,
    down_hbm,
    ids_hbm,
    weight_hbm,
    qbase_hbm,
    kbase_hbm,
    vbase_hbm,
    upq_hbm,
    upk_hbm,
    upv_hbm,
    inverse_hbm,
    out_ref,
    act,
    down,
    ids_ref,
    weight_ref,
    qbase,
    kbase,
    vbase,
    upq,
    upk,
    upv,
    inverse_ref,
    low_send,
    low_recv,
    kv,
    qs,
    top,
    total,
    accum,
    cos_tab,
    sin_tab,
    in_sems,
    low_send_sems,
    low_recv_sems,
    lane_send_sems,
    cross_send_sems,
    recv_sems,
):
    ctx = lax.axis_index("ctx")
    head = lax.axis_index("head")
    z = ctx // 2
    x = ctx % 2
    n_z = n_ctx // 2
    rows, features = act.shape
    local_kv = kbase.shape[1] // HD
    group = qbase.shape[1] // HD // local_kv
    other = 2 * z + 1 - x

    part = features // CHUNKS
    loads = [pltpu.make_async_copy(act_hbm, act, in_sems.at[0])]
    for i in range(CHUNKS):
        piece = pl.ds(i * part, part)
        loads.append(pltpu.make_async_copy(down_hbm.at[piece], down.at[piece], in_sems.at[1 + i]))
    rest = [
        pltpu.make_async_copy(src, dst, in_sems.at[1 + CHUNKS + i])
        for i, (src, dst) in enumerate(
            ((ids_hbm, ids_ref), (weight_hbm, weight_ref), (inverse_hbm, inverse_ref), (kbase_hbm, kbase), (vbase_hbm, vbase), (upk_hbm, upk), (upv_hbm, upv), (qbase_hbm, qbase), (upq_hbm, upq))
        )
    ]
    small, rest = rest[:3], rest[3:]
    for load in small + loads + rest:
        load.start()

    barrier = pltpu.get_barrier_semaphore()
    for step in range(1, n_head):
        pl.semaphore_signal(
            barrier, inc=1, device_id={"ctx": ctx, "head": lax.rem(head + step, n_head)}, device_id_type=MESH
        )
    pl.semaphore_signal(barrier, inc=1, device_id={"ctx": other, "head": head}, device_id_type=MESH)

    @pl.when(z > 0)
    def _():
        pl.semaphore_signal(barrier, inc=1, device_id={"ctx": ctx - 2, "head": head}, device_id_type=MESH)

    @pl.when(z < n_z - 1)
    def _():
        pl.semaphore_signal(barrier, inc=1, device_id={"ctx": ctx + 2, "head": head}, device_id_type=MESH)

    loads[0].wait()
    low = None
    for i in range(CHUNKS):
        loads[1 + i].wait()
        piece = pl.ds(i * part, part)
        term = jnp.dot(act[:, piece], down[piece, :], preferred_element_type=jnp.float32)
        low = term if low is None else low + term

    for load in small:
        load.wait()
    lane = lax.broadcasted_iota(jnp.int32, (rows, HD), 1)
    group_of = lane // RANK
    group_value = group_of.astype(jnp.float32)
    masks = []
    for j in range(2):
        chosen = columns(ids_ref[j : j + 1, :].astype(jnp.float32), rows)
        masks.append((chosen == group_value, chosen == group_value + 4.0))
    packs = []
    for p in range(3):
        for j in range(2):
            first, second = masks[j]
            left = low[:, p * SPAN : p * SPAN + HD]
            right = low[:, p * SPAN + HD : (p + 1) * SPAN]
            packs.append(spread(jnp.where(first, left, jnp.where(second, right, 0.0))))
    half = rows // 2
    upper = jnp.where(
        group_of == 0, packs[2], jnp.where(group_of == 1, packs[3], jnp.where(group_of == 2, packs[4], packs[5]))
    )
    half_group = group_of[:half]
    lower = jnp.where(
        half_group == 0,
        packs[0][:half],
        jnp.where(half_group == 1, packs[1][:half], jnp.where(half_group == 2, packs[0][half:], packs[1][half:])),
    )
    compact = jnp.concatenate([upper, lower], axis=0)
    low_send[...] = compact.astype(jnp.bfloat16)

    neighbours = n_head + (z > 0).astype(jnp.int32) + (z < n_z - 1).astype(jnp.int32)
    pl.semaphore_wait(barrier, neighbours)

    low_copies = []
    for step in range(n_head - 1, 0, -1):
        peer = lax.rem(head + step, n_head)
        copy = pltpu.make_async_remote_copy(
            src_ref=low_send,
            dst_ref=low_recv.at[head],
            send_sem=low_send_sems.at[step],
            recv_sem=low_recv_sems.at[head],
            device_id={"ctx": ctx, "head": peer},
            device_id_type=MESH,
        )
        copy.start()
        low_copies.append(copy)

    spot = lax.broadcasted_iota(jnp.int32, (rows, HD), 0) + ctx * rows
    angles = spot.astype(jnp.float32) * inverse_ref[...]
    cos_tab[...] = jnp.cos(angles)
    sine = jnp.sin(angles)
    sin_tab[...] = jnp.where(lane < HD // 2, -sine, sine)

    for load in rest:
        load.wait()
    for step in range(1, n_head):
        peer = lax.rem(head + step, n_head)
        pltpu.make_async_copy(low_recv.at[peer], low_recv.at[peer], low_recv_sems.at[peer]).wait()
        compact = compact + low_recv[peer].astype(jnp.float32)

    upper, lower = compact[:rows], compact[rows:]
    pieces = [
        jnp.concatenate(
            [
                spread(jnp.where(half_group == j, lower, 0.0)),
                spread(jnp.where(half_group == j + 2, lower, 0.0)),
            ],
            axis=0,
        )
        for j in range(2)
    ]
    pieces += [spread(jnp.where(group_of == k, upper, 0.0)) for k in range(4)]

    shares = [columns(weight_ref[j : j + 1, :], rows) for j in range(2)]

    def gated_of(p):
        first = shares[0] * pieces[2 * p]
        second = shares[1] * pieces[2 * p + 1]
        sides = [
            jnp.where(masks[0][side], first, jnp.where(masks[1][side], second, 0.0)) for side in range(2)
        ]
        return jnp.concatenate(sides, axis=1).astype(jnp.bfloat16)

    def rotated(values):
        return (values * cos_tab[...] + roll_lanes(values, HD // 2) * sin_tab[...]).astype(jnp.bfloat16)

    key_raw = kbase[...].astype(jnp.float32) + jnp.dot(gated_of(1), upk[...], preferred_element_type=jnp.float32)
    for g in range(local_kv):
        kv[ctx, g, :, :HD] = rotated(key_raw[:, g * HD : (g + 1) * HD])
    value = vbase[...].astype(jnp.float32) + jnp.dot(gated_of(2), upv[...], preferred_element_type=jnp.float32)
    for g in range(local_kv):
        kv[ctx, g, :, HD:] = value[:, g * HD : (g + 1) * HD].astype(jnp.bfloat16)

    def lane_copy(block, g):
        return pltpu.make_async_remote_copy(
            src_ref=kv.at[block, g],
            dst_ref=kv.at[block, g],
            send_sem=lane_send_sems.at[block, g],
            recv_sem=recv_sems.at[block, g],
            device_id={"ctx": lax.rem(ctx + 2, n_ctx), "head": head},
            device_id_type=MESH,
        )

    def cross_copy(block, g):
        return pltpu.make_async_remote_copy(
            src_ref=kv.at[block, g],
            dst_ref=kv.at[block, g],
            send_sem=cross_send_sems.at[block, g],
            recv_sem=recv_sems.at[block, g],
            device_id={"ctx": other, "head": head},
            device_id_type=MESH,
        )

    last = local_kv - 1

    def crosses_own(g):
        return jnp.logical_or(x == 0, z == 0) if g == last else x == 0

    def arrived(block, g):
        pltpu.make_async_copy(kv.at[block, g], kv.at[block, g], recv_sems.at[block, g]).wait()

    for g in range(local_kv):

        @pl.when(crosses_own(g))
        def _():
            cross_copy(ctx, g).start()

        @pl.when(z < n_z - 1)
        def _():
            lane_copy(ctx, g).start()

    gated = gated_of(0)
    for g in range(local_kv):
        for h in range(group):
            cols = pl.ds((g * group + h) * HD, HD)
            raw = qbase[:, cols].astype(jnp.float32) + jnp.dot(
                gated, upq[:, cols], preferred_element_type=jnp.float32
            )
            qs[g, h * rows : (h + 1) * rows, :] = rotated(raw)

    factor = math.log2(math.e) / math.sqrt(HD)
    strip = 2 * rows

    def attend(block, count, diagonal, g):
        keys = kv[pl.ds(block, count), g, :, :HD].reshape(count * rows, HD)
        vals = kv[pl.ds(block, count), g, :, HD:].reshape(count * rows, HD)
        for c in range(group * rows // strip):
            span = pl.ds(c * strip, strip)
            scores = (
                lax.dot_general(
                    qs[g, span, :], keys, (((1,), (1,)), ((), ())), preferred_element_type=jnp.float32
                )
                * factor
            )
            if diagonal:
                row = lax.broadcasted_iota(jnp.int32, (strip, rows), 0) % rows
                col = lax.broadcasted_iota(jnp.int32, (strip, rows), 1)
                scores = jnp.where(row >= col, scores, MASKED)
            peak = jnp.max(scores, axis=1, keepdims=True)
            if diagonal:
                new_top = jnp.broadcast_to(peak, (strip, HD))
            else:
                old_top = top[g, span, :]
                new_top = jnp.maximum(old_top, peak)
                shrink = jnp.exp2(old_top - new_top)
            top[g, span, :] = new_top
            sums = None
            expos = []
            for k in range(count):
                expo = jnp.exp2(scores[:, k * rows : (k + 1) * rows] - new_top)
                sums = expo if sums is None else sums + expo
                expos.append(expo.astype(jnp.bfloat16))
            expo = expos[0] if count == 1 else jnp.concatenate(expos, axis=1)
            summed = jnp.dot(expo, vals, preferred_element_type=jnp.float32)
            if diagonal:
                total[g, span, :] = sums
                accum[g, span, :] = summed
            else:
                total[g, span, :] = total[g, span, :] * shrink + sums
                accum[g, span, :] = accum[g, span, :] * shrink + summed

    def send_on(block, g):
        @pl.when(z < n_z - 1)
        def _():
            lane_copy(block, g).start()

    def pass_on(block, g, is_first):
        arrived(block, g)
        send_on(block, g)
        if g == last:

            @pl.when(is_first)
            def _():
                arrived(block + other - ctx, g)
                send_on(block + other - ctx, g)

            @pl.when(jnp.logical_not(is_first))
            def _():
                cross_copy(block, g).start()

        else:
            cross_copy(block, g).start()

    for g in range(local_kv):
        attend(ctx, 1, True, g)

    for g in range(local_kv):

        @pl.when(z > 0)
        def _():
            pass_on(ctx - 2, g, z == 1)

        @pl.when(x == 1)
        def _():
            arrived(ctx - 1, g)
            if g == last:

                @pl.when(z == 0)
                def _():
                    send_on(ctx - 1, g)

            attend(ctx - 1, 1, False, g)

    @pl.when(jnp.logical_and(x == 0, z == 0))
    def _():
        arrived(other, last)
        send_on(other, last)

    def pair_step(step, carry):
        for g in range(local_kv):

            @pl.when(step < z)
            def _():
                pass_on(ctx - 2 * step - 2, g, step + 1 == z)

            if g == last:

                @pl.when(step < z)
                def _():
                    arrived(other - 2 * step, g)

            else:
                arrived(other - 2 * step, g)
            attend(2 * (z - step), 2, False, g)
        return carry

    lax.fori_loop(1, z + 1, pair_step, 0)

    for g in range(local_kv):
        for h in range(group):
            span = pl.ds(h * rows, rows)
            whole = jnp.sum(total[g, span, :], axis=1, keepdims=True)
            cols = pl.ds((g * group + h) * HD, HD)
            out_ref[:, cols] = (accum[g, span, :] / whole).astype(jnp.bfloat16)

    for copy in low_copies:
        copy.wait_send()

    for g in range(local_kv):

        @pl.when(crosses_own(g))
        def _():
            cross_copy(ctx, g).wait_send()

        @pl.when(z < n_z - 1)
        def _():
            lane_copy(ctx, g).wait_send()

    def drain(step, carry):
        block = ctx - 2 * step
        for g in range(local_kv):

            @pl.when(z < n_z - 1)
            def _():
                lane_copy(block, g).wait_send()

            if g == last:

                @pl.when(step < z)
                def _():
                    cross_copy(block, g).wait_send()

            else:
                cross_copy(block, g).wait_send()

        return carry

    lax.fori_loop(1, z + 1, drain, 0)

    @pl.when(z < n_z - 1)
    def _():
        lane_copy(1 - x, last).wait_send()


def on_device(
    n_ctx,
    n_head,
    activations,
    adapter_down,
    adapter_ids,
    adapter_weight,
    query_base,
    key_base,
    value_base,
    up_query,
    up_key,
    up_value,
):
    rows = activations.shape[0]
    width = query_base.shape[1]
    kv_width = key_base.shape[1]
    local_kv = kv_width // HD
    stacked = rows * (width // kv_width)
    exponent = np.arange(HD // 2, dtype=np.float32) * np.float32(-2.0 * math.log(ROPE_BASE) / HD)
    inverse = np.exp(np.concatenate([exponent, exponent])).astype(np.float32)[None, :]
    bf16, f32 = jnp.bfloat16, jnp.float32
    adapter_ids, adapter_weight = adapter_ids.T, adapter_weight.T
    big = (activations, adapter_down, adapter_ids, adapter_weight, query_base, key_base, value_base, up_query, up_key, up_value, inverse)
    anywhere = pl.BlockSpec(memory_space=pl.ANY)
    local = pl.BlockSpec(memory_space=pltpu.VMEM)
    return pl.pallas_call(
        functools.partial(kernel, n_ctx, n_head),
        out_shape=jax.ShapeDtypeStruct((rows, width), bf16),
        in_specs=[anywhere] * 11,
        out_specs=local,
        scratch_shapes=[pltpu.VMEM(array.shape, array.dtype) for array in big]
        + [
            pltpu.VMEM((rows + rows // 2, HD), bf16),
            pltpu.VMEM((n_head, rows + rows // 2, HD), bf16),
            pltpu.VMEM((n_ctx, local_kv, rows, 2 * HD), bf16),
            pltpu.VMEM((local_kv, stacked, HD), bf16),
            pltpu.VMEM((local_kv, stacked, HD), f32),
            pltpu.VMEM((local_kv, stacked, HD), f32),
            pltpu.VMEM((local_kv, stacked, HD), f32),
            pltpu.VMEM((rows, HD), f32),
            pltpu.VMEM((rows, HD), f32),
            pltpu.SemaphoreType.DMA((10 + CHUNKS,)),
            pltpu.SemaphoreType.DMA((n_head,)),
            pltpu.SemaphoreType.DMA((n_head,)),
            pltpu.SemaphoreType.DMA((n_ctx, local_kv)),
            pltpu.SemaphoreType.DMA((n_ctx, local_kv)),
            pltpu.SemaphoreType.DMA((n_ctx, local_kv)),
        ],
        compiler_params=pltpu.CompilerParams(
            collective_id=0, has_side_effects=True, vmem_limit_bytes=63 * 1024 * 1024
        ),
        name="lora_attention",
    )(
        activations,
        adapter_down,
        adapter_ids,
        adapter_weight,
        query_base,
        key_base,
        value_base,
        up_query,
        up_key,
        up_value,
        inverse,
    )


def solution(mesh):
    in_specs = (
        P("ctx", "head"),
        P("head", None),
        P("ctx", None),
        P("ctx", None),
        P("ctx", "head"),
        P("ctx", "head"),
        P("ctx", "head"),
        P(None, "head"),
        P(None, "head"),
        P(None, "head"),
    )
    return jax.shard_map(
        functools.partial(on_device, mesh.shape["ctx"], mesh.shape["head"]),
        mesh=mesh,
        in_specs=in_specs,
        out_specs=P("ctx", "head"),
        check_vma=False,
    )
```

```python
import functools
import math

import jax
import jax.numpy as jnp
import numpy as np
from jax import lax
from jax.experimental import pallas as pl
from jax.experimental.pallas import tpu as pltpu
from jax.sharding import PartitionSpec as P

HD = 128
ADAPTERS = 8
RANK = 32
SPAN = ADAPTERS * RANK
ROPE_BASE = 500000.0
MASKED = -1e30
MESH = pl.DeviceIdType.MESH
CHUNKS = 4


def roll_lanes(values, shift):
    return pltpu.roll(values, shift, 1)


def spread(values):
    values = values + roll_lanes(values, 64)
    return values + roll_lanes(values, 32)


def columns(row, rows):
    return jnp.broadcast_to(row, (HD, rows)).T


def kernel(
    n_ctx,
    n_head,
    act_hbm,
    down_hbm,
    ids_hbm,
    weight_hbm,
    qbase_hbm,
    kbase_hbm,
    vbase_hbm,
    upq_hbm,
    upk_hbm,
    upv_hbm,
    inverse_hbm,
    out_ref,
    act,
    down,
    ids_ref,
    weight_ref,
    qbase,
    kbase,
    vbase,
    upq,
    upk,
    upv,
    inverse_ref,
    low_send,
    low_recv,
    kv,
    qs,
    top,
    total,
    accum,
    cos_tab,
    sin_tab,
    in_sems,
    low_send_sems,
    low_recv_sems,
    lane_send_sems,
    cross_send_sems,
    recv_sems,
):
    ctx = lax.axis_index("ctx")
    head = lax.axis_index("head")
    z = ctx // 2
    x = ctx % 2
    n_z = n_ctx // 2
    rows, features = act.shape
    local_kv = kbase.shape[1] // HD
    group = qbase.shape[1] // HD // local_kv
    other = 2 * z + 1 - x

    part = features // CHUNKS
    loads = [pltpu.make_async_copy(act_hbm, act, in_sems.at[0])]
    for i in range(CHUNKS):
        piece = pl.ds(i * part, part)
        loads.append(pltpu.make_async_copy(down_hbm.at[piece], down.at[piece], in_sems.at[1 + i]))
    rest = [
        pltpu.make_async_copy(src, dst, in_sems.at[1 + CHUNKS + i])
        for i, (src, dst) in enumerate(
            ((ids_hbm, ids_ref), (weight_hbm, weight_ref), (inverse_hbm, inverse_ref), (kbase_hbm, kbase), (vbase_hbm, vbase), (upk_hbm, upk), (upv_hbm, upv), (qbase_hbm, qbase), (upq_hbm, upq))
        )
    ]
    small, rest = rest[:3], rest[3:]
    for load in small + loads + rest:
        load.start()

    barrier = pltpu.get_barrier_semaphore()
    for step in range(1, n_head):
        pl.semaphore_signal(
            barrier, inc=1, device_id={"ctx": ctx, "head": lax.rem(head + step, n_head)}, device_id_type=MESH
        )
    pl.semaphore_signal(barrier, inc=1, device_id={"ctx": other, "head": head}, device_id_type=MESH)

    @pl.when(z > 0)
    def _():
        pl.semaphore_signal(barrier, inc=1, device_id={"ctx": ctx - 2, "head": head}, device_id_type=MESH)

    @pl.when(z < n_z - 1)
    def _():
        pl.semaphore_signal(barrier, inc=1, device_id={"ctx": ctx + 2, "head": head}, device_id_type=MESH)

    loads[0].wait()
    low = None
    for i in range(CHUNKS):
        loads[1 + i].wait()
        piece = pl.ds(i * part, part)
        term = jnp.dot(act[:, piece], down[piece, :], preferred_element_type=jnp.float32)
        low = term if low is None else low + term

    for load in small:
        load.wait()
    lane = lax.broadcasted_iota(jnp.int32, (rows, HD), 1)
    group_of = lane // RANK
    group_value = group_of.astype(jnp.float32)
    masks = []
    for j in range(2):
        chosen = columns(ids_ref[j : j + 1, :].astype(jnp.float32), rows)
        masks.append((chosen == group_value, chosen == group_value + 4.0))
    packs = []
    for p in range(3):
        for j in range(2):
            first, second = masks[j]
            left = low[:, p * SPAN : p * SPAN + HD]
            right = low[:, p * SPAN + HD : (p + 1) * SPAN]
            packs.append(spread(jnp.where(first, left, jnp.where(second, right, 0.0))))
    half = rows // 2
    upper = jnp.where(
        group_of == 0, packs[2], jnp.where(group_of == 1, packs[3], jnp.where(group_of == 2, packs[4], packs[5]))
    )
    half_group = group_of[:half]
    lower = jnp.where(
        half_group == 0,
        packs[0][:half],
        jnp.where(half_group == 1, packs[1][:half], jnp.where(half_group == 2, packs[0][half:], packs[1][half:])),
    )
    compact = jnp.concatenate([upper, lower], axis=0)
    low_send[...] = compact.astype(jnp.bfloat16)

    neighbours = n_head + (z > 0).astype(jnp.int32) + (z < n_z - 1).astype(jnp.int32)
    pl.semaphore_wait(barrier, neighbours)

    low_copies = []
    for step in range(n_head - 1, 0, -1):
        peer = lax.rem(head + step, n_head)
        copy = pltpu.make_async_remote_copy(
            src_ref=low_send,
            dst_ref=low_recv.at[head],
            send_sem=low_send_sems.at[step],
            recv_sem=low_recv_sems.at[head],
            device_id={"ctx": ctx, "head": peer},
            device_id_type=MESH,
        )
        copy.start()
        low_copies.append(copy)

    spot = lax.broadcasted_iota(jnp.int32, (rows, HD), 0) + ctx * rows
    angles = spot.astype(jnp.float32) * inverse_ref[...]
    cos_tab[...] = jnp.cos(angles)
    sine = jnp.sin(angles)
    sin_tab[...] = jnp.where(lane < HD // 2, -sine, sine)

    for load in rest:
        load.wait()
    for step in range(1, n_head):
        peer = lax.rem(head + step, n_head)
        pltpu.make_async_copy(low_recv.at[peer], low_recv.at[peer], low_recv_sems.at[peer]).wait()
        compact = compact + low_recv[peer].astype(jnp.float32)

    upper, lower = compact[:rows], compact[rows:]
    pieces = [
        jnp.concatenate(
            [
                spread(jnp.where(half_group == j, lower, 0.0)),
                spread(jnp.where(half_group == j + 2, lower, 0.0)),
            ],
            axis=0,
        )
        for j in range(2)
    ]
    pieces += [spread(jnp.where(group_of == k, upper, 0.0)) for k in range(4)]

    shares = [columns(weight_ref[j : j + 1, :], rows) for j in range(2)]

    def gated_of(p):
        first = shares[0] * pieces[2 * p]
        second = shares[1] * pieces[2 * p + 1]
        sides = [
            jnp.where(masks[0][side], first, jnp.where(masks[1][side], second, 0.0)) for side in range(2)
        ]
        return jnp.concatenate(sides, axis=1).astype(jnp.bfloat16)

    def rotated(values):
        return (values * cos_tab[...] + roll_lanes(values, HD // 2) * sin_tab[...]).astype(jnp.bfloat16)

    key_raw = kbase[...].astype(jnp.float32) + jnp.dot(gated_of(1), upk[...], preferred_element_type=jnp.float32)
    for g in range(local_kv):
        kv[ctx, g, :, :HD] = rotated(key_raw[:, g * HD : (g + 1) * HD])
    value = vbase[...].astype(jnp.float32) + jnp.dot(gated_of(2), upv[...], preferred_element_type=jnp.float32)
    for g in range(local_kv):
        kv[ctx, g, :, HD:] = value[:, g * HD : (g + 1) * HD].astype(jnp.bfloat16)

    def lane_copy(block, g):
        return pltpu.make_async_remote_copy(
            src_ref=kv.at[block, g],
            dst_ref=kv.at[block, g],
            send_sem=lane_send_sems.at[block, g],
            recv_sem=recv_sems.at[block, g],
            device_id={"ctx": lax.rem(ctx + 2, n_ctx), "head": head},
            device_id_type=MESH,
        )

    def cross_copy(block, g):
        return pltpu.make_async_remote_copy(
            src_ref=kv.at[block, g],
            dst_ref=kv.at[block, g],
            send_sem=cross_send_sems.at[block, g],
            recv_sem=recv_sems.at[block, g],
            device_id={"ctx": other, "head": head},
            device_id_type=MESH,
        )

    last = local_kv - 1

    def crosses_own(g):
        return jnp.logical_or(x == 0, z == 0) if g == last else x == 0

    def arrived(block, g):
        pltpu.make_async_copy(kv.at[block, g], kv.at[block, g], recv_sems.at[block, g]).wait()

    for g in range(local_kv):

        @pl.when(crosses_own(g))
        def _():
            cross_copy(ctx, g).start()

        @pl.when(z < n_z - 1)
        def _():
            lane_copy(ctx, g).start()

    gated = gated_of(0)
    for g in range(local_kv):
        for h in range(group):
            cols = pl.ds((g * group + h) * HD, HD)
            raw = qbase[:, cols].astype(jnp.float32) + jnp.dot(
                gated, upq[:, cols], preferred_element_type=jnp.float32
            )
            qs[g, h * rows : (h + 1) * rows, :] = rotated(raw)

    factor = math.log2(math.e) / math.sqrt(HD)
    strip = 2 * rows

    def attend(block, count, diagonal, g):
        keys = kv[pl.ds(block, count), g, :, :HD].reshape(count * rows, HD)
        vals = kv[pl.ds(block, count), g, :, HD:].reshape(count * rows, HD)
        for c in range(group * rows // strip):
            span = pl.ds(c * strip, strip)
            scores = (
                lax.dot_general(
                    qs[g, span, :], keys, (((1,), (1,)), ((), ())), preferred_element_type=jnp.float32
                )
                * factor
            )
            if diagonal:
                row = lax.broadcasted_iota(jnp.int32, (strip, rows), 0) % rows
                col = lax.broadcasted_iota(jnp.int32, (strip, rows), 1)
                scores = jnp.where(row >= col, scores, MASKED)
            peak = jnp.max(scores, axis=1, keepdims=True)
            if diagonal:
                new_top = jnp.broadcast_to(peak, (strip, HD))
            else:
                old_top = top[g, span, :]
                new_top = jnp.maximum(old_top, peak)
                shrink = jnp.exp2(old_top - new_top)
            top[g, span, :] = new_top
            sums = None
            expos = []
            for k in range(count):
                expo = jnp.exp2(scores[:, k * rows : (k + 1) * rows] - new_top)
                sums = expo if sums is None else sums + expo
                expos.append(expo.astype(jnp.bfloat16))
            expo = expos[0] if count == 1 else jnp.concatenate(expos, axis=1)
            summed = jnp.dot(expo, vals, preferred_element_type=jnp.float32)
            if diagonal:
                total[g, span, :] = sums
                accum[g, span, :] = summed
            else:
                total[g, span, :] = total[g, span, :] * shrink + sums
                accum[g, span, :] = accum[g, span, :] * shrink + summed

    def send_on(block, g):
        @pl.when(z < n_z - 1)
        def _():
            lane_copy(block, g).start()

    def pass_on(block, g, is_first):
        arrived(block, g)
        send_on(block, g)
        if g == last:

            @pl.when(is_first)
            def _():
                arrived(block + other - ctx, g)
                send_on(block + other - ctx, g)

            @pl.when(jnp.logical_not(is_first))
            def _():
                cross_copy(block, g).start()

        else:
            cross_copy(block, g).start()

    for g in range(local_kv):

        @pl.when(z > 0)
        def _():
            pass_on(ctx - 2, g, z == 1)

        attend(ctx, 1, True, g)

    for g in range(local_kv):

        @pl.when(x == 1)
        def _():
            arrived(ctx - 1, g)
            if g == last:

                @pl.when(z == 0)
                def _():
                    send_on(ctx - 1, g)

            attend(ctx - 1, 1, False, g)

    @pl.when(jnp.logical_and(x == 0, z == 0))
    def _():
        arrived(other, last)
        send_on(other, last)

    def pair_step(step, carry):
        for g in range(local_kv):

            @pl.when(step < z)
            def _():
                pass_on(ctx - 2 * step - 2, g, step + 1 == z)

            if g == last:

                @pl.when(step < z)
                def _():
                    arrived(other - 2 * step, g)

            else:
                arrived(other - 2 * step, g)
            attend(2 * (z - step), 2, False, g)
        return carry

    lax.fori_loop(1, z + 1, pair_step, 0)

    for g in range(local_kv):
        for h in range(group):
            span = pl.ds(h * rows, rows)
            whole = jnp.sum(total[g, span, :], axis=1, keepdims=True)
            cols = pl.ds((g * group + h) * HD, HD)
            out_ref[:, cols] = (accum[g, span, :] / whole).astype(jnp.bfloat16)

    for copy in low_copies:
        copy.wait_send()

    for g in range(local_kv):

        @pl.when(crosses_own(g))
        def _():
            cross_copy(ctx, g).wait_send()

        @pl.when(z < n_z - 1)
        def _():
            lane_copy(ctx, g).wait_send()

    def drain(step, carry):
        block = ctx - 2 * step
        for g in range(local_kv):

            @pl.when(z < n_z - 1)
            def _():
                lane_copy(block, g).wait_send()

            if g == last:

                @pl.when(step < z)
                def _():
                    cross_copy(block, g).wait_send()

            else:
                cross_copy(block, g).wait_send()

        return carry

    lax.fori_loop(1, z + 1, drain, 0)

    @pl.when(z < n_z - 1)
    def _():
        lane_copy(1 - x, last).wait_send()


def on_device(
    n_ctx,
    n_head,
    activations,
    adapter_down,
    adapter_ids,
    adapter_weight,
    query_base,
    key_base,
    value_base,
    up_query,
    up_key,
    up_value,
):
    rows = activations.shape[0]
    width = query_base.shape[1]
    kv_width = key_base.shape[1]
    local_kv = kv_width // HD
    stacked = rows * (width // kv_width)
    exponent = np.arange(HD // 2, dtype=np.float32) * np.float32(-2.0 * math.log(ROPE_BASE) / HD)
    inverse = np.exp(np.concatenate([exponent, exponent])).astype(np.float32)[None, :]
    bf16, f32 = jnp.bfloat16, jnp.float32
    adapter_ids, adapter_weight = adapter_ids.T, adapter_weight.T
    big = (activations, adapter_down, adapter_ids, adapter_weight, query_base, key_base, value_base, up_query, up_key, up_value, inverse)
    anywhere = pl.BlockSpec(memory_space=pl.ANY)
    local = pl.BlockSpec(memory_space=pltpu.VMEM)
    return pl.pallas_call(
        functools.partial(kernel, n_ctx, n_head),
        out_shape=jax.ShapeDtypeStruct((rows, width), bf16),
        in_specs=[anywhere] * 11,
        out_specs=local,
        scratch_shapes=[pltpu.VMEM(array.shape, array.dtype) for array in big]
        + [
            pltpu.VMEM((rows + rows // 2, HD), bf16),
            pltpu.VMEM((n_head, rows + rows // 2, HD), bf16),
            pltpu.VMEM((n_ctx, local_kv, rows, 2 * HD), bf16),
            pltpu.VMEM((local_kv, stacked, HD), bf16),
            pltpu.VMEM((local_kv, stacked, HD), f32),
            pltpu.VMEM((local_kv, stacked, HD), f32),
            pltpu.VMEM((local_kv, stacked, HD), f32),
            pltpu.VMEM((rows, HD), f32),
            pltpu.VMEM((rows, HD), f32),
            pltpu.SemaphoreType.DMA((10 + CHUNKS,)),
            pltpu.SemaphoreType.DMA((n_head,)),
            pltpu.SemaphoreType.DMA((n_head,)),
            pltpu.SemaphoreType.DMA((n_ctx, local_kv)),
            pltpu.SemaphoreType.DMA((n_ctx, local_kv)),
            pltpu.SemaphoreType.DMA((n_ctx, local_kv)),
        ],
        compiler_params=pltpu.CompilerParams(
            collective_id=0, has_side_effects=True, vmem_limit_bytes=63 * 1024 * 1024
        ),
        name="lora_attention",
    )(
        activations,
        adapter_down,
        adapter_ids,
        adapter_weight,
        query_base,
        key_base,
        value_base,
        up_query,
        up_key,
        up_value,
        inverse,
    )


def solution(mesh):
    in_specs = (
        P("ctx", "head"),
        P("head", None),
        P("ctx", None),
        P("ctx", None),
        P("ctx", "head"),
        P("ctx", "head"),
        P("ctx", "head"),
        P(None, "head"),
        P(None, "head"),
        P(None, "head"),
    )
    return jax.shard_map(
        functools.partial(on_device, mesh.shape["ctx"], mesh.shape["head"]),
        mesh=mesh,
        in_specs=in_specs,
        out_specs=P("ctx", "head"),
        check_vma=False,
    )
```

```python
import functools
import math

import jax
import jax.numpy as jnp
import numpy as np
from jax import lax
from jax.experimental import pallas as pl
from jax.experimental.pallas import tpu as pltpu
from jax.sharding import PartitionSpec as P

HD = 128
ADAPTERS = 8
RANK = 32
SPAN = ADAPTERS * RANK
ROPE_BASE = 500000.0
MASKED = -1e30
MESH = pl.DeviceIdType.MESH
CHUNKS = 4


def roll_lanes(values, shift):
    return pltpu.roll(values, shift, 1)


def spread(values):
    values = values + roll_lanes(values, 64)
    return values + roll_lanes(values, 32)


def columns(row, rows):
    return jnp.broadcast_to(row, (HD, rows)).T


def kernel(
    n_ctx,
    n_head,
    act_hbm,
    down_hbm,
    ids_hbm,
    weight_hbm,
    qbase_hbm,
    kbase_hbm,
    vbase_hbm,
    upq_hbm,
    upk_hbm,
    upv_hbm,
    inverse_hbm,
    out_ref,
    act,
    down,
    ids_ref,
    weight_ref,
    qbase,
    kbase,
    vbase,
    upq,
    upk,
    upv,
    inverse_ref,
    low_send,
    low_recv,
    kv,
    qs,
    top,
    total,
    accum,
    cos_tab,
    sin_tab,
    in_sems,
    low_send_sems,
    low_recv_sems,
    lane_send_sems,
    cross_send_sems,
    recv_sems,
):
    ctx = lax.axis_index("ctx")
    head = lax.axis_index("head")
    z = ctx // 2
    x = ctx % 2
    n_z = n_ctx // 2
    rows, features = act.shape
    local_kv = kbase.shape[1] // HD
    group = qbase.shape[1] // HD // local_kv
    other = 2 * z + 1 - x

    part = features // CHUNKS
    loads = [pltpu.make_async_copy(act_hbm, act, in_sems.at[0])]
    for i in range(CHUNKS):
        piece = pl.ds(i * part, part)
        loads.append(pltpu.make_async_copy(down_hbm.at[piece], down.at[piece], in_sems.at[1 + i]))
    rest = [
        pltpu.make_async_copy(src, dst, in_sems.at[1 + CHUNKS + i])
        for i, (src, dst) in enumerate(
            ((ids_hbm, ids_ref), (weight_hbm, weight_ref), (inverse_hbm, inverse_ref), (kbase_hbm, kbase), (vbase_hbm, vbase), (upk_hbm, upk), (upv_hbm, upv), (qbase_hbm, qbase), (upq_hbm, upq))
        )
    ]
    small, rest = rest[:3], rest[3:]
    for load in small + loads + rest:
        load.start()

    barrier = pltpu.get_barrier_semaphore()
    for step in range(1, n_head):
        pl.semaphore_signal(
            barrier, inc=1, device_id={"ctx": ctx, "head": lax.rem(head + step, n_head)}, device_id_type=MESH
        )
    pl.semaphore_signal(barrier, inc=1, device_id={"ctx": other, "head": head}, device_id_type=MESH)

    @pl.when(z > 0)
    def _():
        pl.semaphore_signal(barrier, inc=1, device_id={"ctx": ctx - 2, "head": head}, device_id_type=MESH)

    @pl.when(z < n_z - 1)
    def _():
        pl.semaphore_signal(barrier, inc=1, device_id={"ctx": ctx + 2, "head": head}, device_id_type=MESH)

    loads[0].wait()
    low = None
    for i in range(CHUNKS):
        loads[1 + i].wait()
        piece = pl.ds(i * part, part)
        term = jnp.dot(act[:, piece], down[piece, :], preferred_element_type=jnp.float32)
        low = term if low is None else low + term

    for load in small:
        load.wait()
    lane = lax.broadcasted_iota(jnp.int32, (rows, HD), 1)
    group_of = lane // RANK
    group_value = group_of.astype(jnp.float32)
    masks = []
    for j in range(2):
        chosen = columns(ids_ref[j : j + 1, :].astype(jnp.float32), rows)
        masks.append((chosen == group_value, chosen == group_value + 4.0))
    packs = []
    for p in range(3):
        for j in range(2):
            first, second = masks[j]
            left = low[:, p * SPAN : p * SPAN + HD]
            right = low[:, p * SPAN + HD : (p + 1) * SPAN]
            packs.append(spread(jnp.where(first, left, jnp.where(second, right, 0.0))))
    half = rows // 2
    upper = jnp.where(
        group_of == 0, packs[2], jnp.where(group_of == 1, packs[3], jnp.where(group_of == 2, packs[4], packs[5]))
    )
    half_group = group_of[:half]
    lower = jnp.where(
        half_group == 0,
        packs[0][:half],
        jnp.where(half_group == 1, packs[1][:half], jnp.where(half_group == 2, packs[0][half:], packs[1][half:])),
    )
    compact = jnp.concatenate([upper, lower], axis=0)
    low_send[...] = compact.astype(jnp.bfloat16)

    neighbours = n_head + (z > 0).astype(jnp.int32) + (z < n_z - 1).astype(jnp.int32)
    pl.semaphore_wait(barrier, neighbours)

    low_copies = []
    for step in range(n_head - 1, 0, -1):
        peer = lax.rem(head + step, n_head)
        copy = pltpu.make_async_remote_copy(
            src_ref=low_send,
            dst_ref=low_recv.at[head],
            send_sem=low_send_sems.at[step],
            recv_sem=low_recv_sems.at[head],
            device_id={"ctx": ctx, "head": peer},
            device_id_type=MESH,
        )
        copy.start()
        low_copies.append(copy)

    spot = lax.broadcasted_iota(jnp.int32, (rows, HD), 0) + ctx * rows
    angles = spot.astype(jnp.float32) * inverse_ref[...]
    cos_tab[...] = jnp.cos(angles)
    sine = jnp.sin(angles)
    sin_tab[...] = jnp.where(lane < HD // 2, -sine, sine)

    for load in rest:
        load.wait()
    for step in range(1, n_head):
        peer = lax.rem(head + step, n_head)
        pltpu.make_async_copy(low_recv.at[peer], low_recv.at[peer], low_recv_sems.at[peer]).wait()
        compact = compact + low_recv[peer].astype(jnp.float32)

    upper, lower = compact[:rows], compact[rows:]
    pieces = [
        jnp.concatenate(
            [
                spread(jnp.where(half_group == j, lower, 0.0)),
                spread(jnp.where(half_group == j + 2, lower, 0.0)),
            ],
            axis=0,
        )
        for j in range(2)
    ]
    pieces += [spread(jnp.where(group_of == k, upper, 0.0)) for k in range(4)]

    shares = [columns(weight_ref[j : j + 1, :], rows) for j in range(2)]

    def gated_of(p):
        first = shares[0] * pieces[2 * p]
        second = shares[1] * pieces[2 * p + 1]
        sides = [
            jnp.where(masks[0][side], first, jnp.where(masks[1][side], second, 0.0)) for side in range(2)
        ]
        return jnp.concatenate(sides, axis=1).astype(jnp.bfloat16)

    def rotated(values):
        return (values * cos_tab[...] + roll_lanes(values, HD // 2) * sin_tab[...]).astype(jnp.bfloat16)

    key_raw = kbase[...].astype(jnp.float32) + jnp.dot(gated_of(1), upk[...], preferred_element_type=jnp.float32)
    for g in range(local_kv):
        kv[ctx, g, :, :HD] = rotated(key_raw[:, g * HD : (g + 1) * HD])
    value = vbase[...].astype(jnp.float32) + jnp.dot(gated_of(2), upv[...], preferred_element_type=jnp.float32)
    for g in range(local_kv):
        kv[ctx, g, :, HD:] = value[:, g * HD : (g + 1) * HD].astype(jnp.bfloat16)

    def lane_copy(block, g):
        return pltpu.make_async_remote_copy(
            src_ref=kv.at[block, g],
            dst_ref=kv.at[block, g],
            send_sem=lane_send_sems.at[block, g],
            recv_sem=recv_sems.at[block, g],
            device_id={"ctx": lax.rem(ctx + 2, n_ctx), "head": head},
            device_id_type=MESH,
        )

    def cross_copy(block, g):
        return pltpu.make_async_remote_copy(
            src_ref=kv.at[block, g],
            dst_ref=kv.at[block, g],
            send_sem=cross_send_sems.at[block, g],
            recv_sem=recv_sems.at[block, g],
            device_id={"ctx": other, "head": head},
            device_id_type=MESH,
        )

    last = local_kv - 1

    def crosses_own(g):
        return jnp.logical_or(x == 0, z == 0) if g == last else x == 0

    def arrived(block, g):
        pltpu.make_async_copy(kv.at[block, g], kv.at[block, g], recv_sems.at[block, g]).wait()

    for g in range(local_kv):

        @pl.when(crosses_own(g))
        def _():
            cross_copy(ctx, g).start()

        @pl.when(z < n_z - 1)
        def _():
            lane_copy(ctx, g).start()

    gated = gated_of(0)
    for g in range(local_kv):
        for h in range(group):
            cols = pl.ds((g * group + h) * HD, HD)
            raw = qbase[:, cols].astype(jnp.float32) + jnp.dot(
                gated, upq[:, cols], preferred_element_type=jnp.float32
            )
            qs[g, h * rows : (h + 1) * rows, :] = rotated(raw)

    factor = math.log2(math.e) / math.sqrt(HD)
    strip = 4 * rows

    def attend(block, count, diagonal, g):
        keys = kv[pl.ds(block, count), g, :, :HD].reshape(count * rows, HD)
        vals = kv[pl.ds(block, count), g, :, HD:].reshape(count * rows, HD)
        for c in range(group * rows // strip):
            span = pl.ds(c * strip, strip)
            scores = (
                lax.dot_general(
                    qs[g, span, :], keys, (((1,), (1,)), ((), ())), preferred_element_type=jnp.float32
                )
                * factor
            )
            if diagonal:
                row = lax.broadcasted_iota(jnp.int32, (strip, rows), 0) % rows
                col = lax.broadcasted_iota(jnp.int32, (strip, rows), 1)
                scores = jnp.where(row >= col, scores, MASKED)
            peak = jnp.max(scores, axis=1, keepdims=True)
            if diagonal:
                new_top = jnp.broadcast_to(peak, (strip, HD))
            else:
                old_top = top[g, span, :]
                new_top = jnp.maximum(old_top, peak)
                shrink = jnp.exp2(old_top - new_top)
            top[g, span, :] = new_top
            sums = None
            expos = []
            for k in range(count):
                expo = jnp.exp2(scores[:, k * rows : (k + 1) * rows] - new_top)
                sums = expo if sums is None else sums + expo
                expos.append(expo.astype(jnp.bfloat16))
            expo = expos[0] if count == 1 else jnp.concatenate(expos, axis=1)
            summed = jnp.dot(expo, vals, preferred_element_type=jnp.float32)
            if diagonal:
                total[g, span, :] = sums
                accum[g, span, :] = summed
            else:
                total[g, span, :] = total[g, span, :] * shrink + sums
                accum[g, span, :] = accum[g, span, :] * shrink + summed

    def send_on(block, g):
        @pl.when(z < n_z - 1)
        def _():
            lane_copy(block, g).start()

    def pass_on(block, g, is_first):
        arrived(block, g)
        send_on(block, g)
        if g == last:

            @pl.when(is_first)
            def _():
                arrived(block + other - ctx, g)
                send_on(block + other - ctx, g)

            @pl.when(jnp.logical_not(is_first))
            def _():
                cross_copy(block, g).start()

        else:
            cross_copy(block, g).start()

    for g in range(local_kv):
        attend(ctx, 1, True, g)

    for g in range(local_kv):

        @pl.when(z > 0)
        def _():
            pass_on(ctx - 2, g, z == 1)

        @pl.when(x == 1)
        def _():
            arrived(ctx - 1, g)
            if g == last:

                @pl.when(z == 0)
                def _():
                    send_on(ctx - 1, g)

            attend(ctx - 1, 1, False, g)

    @pl.when(jnp.logical_and(x == 0, z == 0))
    def _():
        arrived(other, last)
        send_on(other, last)

    def pair_step(step, carry):
        for g in range(local_kv):

            @pl.when(step < z)
            def _():
                pass_on(ctx - 2 * step - 2, g, step + 1 == z)

            if g == last:

                @pl.when(step < z)
                def _():
                    arrived(other - 2 * step, g)

            else:
                arrived(other - 2 * step, g)
            attend(2 * (z - step), 2, False, g)
        return carry

    lax.fori_loop(1, z + 1, pair_step, 0)

    for g in range(local_kv):
        for h in range(group):
            span = pl.ds(h * rows, rows)
            whole = jnp.sum(total[g, span, :], axis=1, keepdims=True)
            cols = pl.ds((g * group + h) * HD, HD)
            out_ref[:, cols] = (accum[g, span, :] / whole).astype(jnp.bfloat16)

    for copy in low_copies:
        copy.wait_send()

    for g in range(local_kv):

        @pl.when(crosses_own(g))
        def _():
            cross_copy(ctx, g).wait_send()

        @pl.when(z < n_z - 1)
        def _():
            lane_copy(ctx, g).wait_send()

    def drain(step, carry):
        block = ctx - 2 * step
        for g in range(local_kv):

            @pl.when(z < n_z - 1)
            def _():
                lane_copy(block, g).wait_send()

            if g == last:

                @pl.when(step < z)
                def _():
                    cross_copy(block, g).wait_send()

            else:
                cross_copy(block, g).wait_send()

        return carry

    lax.fori_loop(1, z + 1, drain, 0)

    @pl.when(z < n_z - 1)
    def _():
        lane_copy(1 - x, last).wait_send()


def on_device(
    n_ctx,
    n_head,
    activations,
    adapter_down,
    adapter_ids,
    adapter_weight,
    query_base,
    key_base,
    value_base,
    up_query,
    up_key,
    up_value,
):
    rows = activations.shape[0]
    width = query_base.shape[1]
    kv_width = key_base.shape[1]
    local_kv = kv_width // HD
    stacked = rows * (width // kv_width)
    exponent = np.arange(HD // 2, dtype=np.float32) * np.float32(-2.0 * math.log(ROPE_BASE) / HD)
    inverse = np.exp(np.concatenate([exponent, exponent])).astype(np.float32)[None, :]
    bf16, f32 = jnp.bfloat16, jnp.float32
    adapter_ids, adapter_weight = adapter_ids.T, adapter_weight.T
    big = (activations, adapter_down, adapter_ids, adapter_weight, query_base, key_base, value_base, up_query, up_key, up_value, inverse)
    anywhere = pl.BlockSpec(memory_space=pl.ANY)
    local = pl.BlockSpec(memory_space=pltpu.VMEM)
    return pl.pallas_call(
        functools.partial(kernel, n_ctx, n_head),
        out_shape=jax.ShapeDtypeStruct((rows, width), bf16),
        in_specs=[anywhere] * 11,
        out_specs=local,
        scratch_shapes=[pltpu.VMEM(array.shape, array.dtype) for array in big]
        + [
            pltpu.VMEM((rows + rows // 2, HD), bf16),
            pltpu.VMEM((n_head, rows + rows // 2, HD), bf16),
            pltpu.VMEM((n_ctx, local_kv, rows, 2 * HD), bf16),
            pltpu.VMEM((local_kv, stacked, HD), bf16),
            pltpu.VMEM((local_kv, stacked, HD), f32),
            pltpu.VMEM((local_kv, stacked, HD), f32),
            pltpu.VMEM((local_kv, stacked, HD), f32),
            pltpu.VMEM((rows, HD), f32),
            pltpu.VMEM((rows, HD), f32),
            pltpu.SemaphoreType.DMA((10 + CHUNKS,)),
            pltpu.SemaphoreType.DMA((n_head,)),
            pltpu.SemaphoreType.DMA((n_head,)),
            pltpu.SemaphoreType.DMA((n_ctx, local_kv)),
            pltpu.SemaphoreType.DMA((n_ctx, local_kv)),
            pltpu.SemaphoreType.DMA((n_ctx, local_kv)),
        ],
        compiler_params=pltpu.CompilerParams(
            collective_id=0, has_side_effects=True, vmem_limit_bytes=63 * 1024 * 1024
        ),
        name="lora_attention",
    )(
        activations,
        adapter_down,
        adapter_ids,
        adapter_weight,
        query_base,
        key_base,
        value_base,
        up_query,
        up_key,
        up_value,
        inverse,
    )


def solution(mesh):
    in_specs = (
        P("ctx", "head"),
        P("head", None),
        P("ctx", None),
        P("ctx", None),
        P("ctx", "head"),
        P("ctx", "head"),
        P("ctx", "head"),
        P(None, "head"),
        P(None, "head"),
        P(None, "head"),
    )
    return jax.shard_map(
        functools.partial(on_device, mesh.shape["ctx"], mesh.shape["head"]),
        mesh=mesh,
        in_specs=in_specs,
        out_specs=P("ctx", "head"),
        check_vma=False,
    )
```
